512 devices in a mesh: sec: 32 (over y, x), term: 16 (over z, core).
Axes of the slice: x: 4, y: 8, z: 8, core: 2. Of those that a mesh axis runs over, the one named last changes fastest.
Arguments:
- psi: bfloat16 [3, 512, 128, 128], P(None, 'sec'), may hold values from -6 to 6
- left_env: bfloat16 [64, 64, 128, 128], P('term', 'sec'), may hold values from -0.5 to 0.5
- right_env: bfloat16 [64, 64, 128, 128], P('term', 'sec'), may hold values from -0.0625 to 0.0625
- left_pick: int32 [512], P('sec'), may hold values from 0 to 1
- right_owner: int32 [512], replicated, may hold values from 0 to 31, as said below
- right_pick: int32 [512], replicated, may hold values from 0 to 1
Outputs:
- sigma: bfloat16 [3, 1024, 128, 128], P(None, 'sec', 'term')
The draws below stay inside these ranges and needn't reach their ends.
Inputs may be any that keep to these rules, and one draw needn't show every extreme that they name: `right_owner`: within the 16 blocks of one device (aligned blocks of the index) each owner appears either 0 or 1 times; some owner appears 1 times in every device's blocks.
All inputs are finite; a program needn't handle non-finite values.
Results may differ from the reference program's by a relative error of at most 0.023.
Values may be sent and summed in bfloat16 or wider, within the bound.
No kernel may reach another device: no remote copies, remote signals or barrier semaphores. Data moves between devices by JAX's collectives and lax.ppermute only.
A program may use at most 128 MiB of HBM per device.

```python
import jax
import jax.numpy as jnp
from jax import lax

B = 128
VECS = 3
PAIR_DEV = 16
LSEC_DEV = 2
RSEC_DEV = 2
TERM_DEV = 4
TERMS = 64
PAIRS = 512
SLOT = 1
RECV_DEV = 32
N_SEC = 32
N_TERM = 16


def draw_right_owner(key, part):
    key = jax.random.fold_in(key, 11)
    groups = PAIRS // PAIR_DEV
    hot = jax.random.randint(jax.random.fold_in(key, 1), (), 0, groups)

    def one_source(source):
        inner = jax.random.fold_in(key, source + 2)
        perm = jax.random.permutation(jax.random.fold_in(inner, 0), groups)
        first = perm[0]
        perm = jnp.where(perm == hot, first, perm).at[0].set(hot)
        chosen = jnp.repeat(perm[:groups // 2], SLOT)
        order = jax.random.permutation(jax.random.fold_in(inner, 1), PAIR_DEV)
        return chosen[order]
    return jax.vmap(one_source)(jnp.arange(groups)).reshape(-1).astype(jnp.int32)


def with_ends(array, rng, least, high):
    place = [jax.random.randint(jax.random.fold_in(rng, axis), (), 0, length) for axis, length in enumerate(array.shape)]
    main_axis = array.shape.index(max(array.shape))
    next_to = place[:main_axis] + [(place[main_axis] + 1) % array.shape[main_axis]] + place[main_axis + 1:]
    return array.at[tuple(place)].set(least).at[tuple(next_to)].set(high)


def block_scale(rng, shape, cuts, least, high):
    level, own = 1.0, jax.random.fold_in(rng, 6)
    for axis_at, blocks in cuts:
        draws = jnp.exp(jax.random.uniform(jax.random.fold_in(own, axis_at), (blocks,), jnp.float32, least / len(cuts), high / len(cuts)))
        level = level * jnp.repeat(draws, shape[axis_at] // blocks).reshape([-1 if axis == axis_at else 1 for axis in range(len(shape))])
    return level


def gaussian(stream_key, dims, scale, bound, split=(), kind=jnp.bfloat16):
    drawn = jax.random.normal(stream_key, dims, jnp.float32) * scale
    if len(split) > 0:
        drawn = block_scale(stream_key, dims, split, -0.22, 0.18) * drawn
    return jnp.clip(drawn, min=-bound, max=bound).astype(kind)


def setup_inputs(seed: int = 0) -> dict:
    key_list = jax.random.split(jax.random.key(seed), 7)
    psi = gaussian(key_list[0], (VECS, PAIRS, B, B), 1.0, 6.0, ((1, 32),))
    left_env = gaussian(key_list[1], (TERMS, LSEC_DEV * N_SEC, B, B), B ** -0.5, 0.5, ((0, 16), (1, 32)))
    right_env = gaussian(key_list[2], (TERMS, RSEC_DEV * N_SEC, B, B), (B * TERMS) ** -0.5, 0.0625, ((0, 16), (1, 32)))
    left_pick = with_ends(jax.random.randint(key_list[3], (PAIRS,), 0, LSEC_DEV), jax.random.fold_in(key_list[3], 1), 0, LSEC_DEV - 1).astype(jnp.int32)
    right_owner = draw_right_owner(jax.random.fold_in(key_list[6], 71), 0)
    right_pick = with_ends(jax.random.randint(key_list[5], (PAIRS,), 0, RSEC_DEV), jax.random.fold_in(key_list[5], 1), 0, RSEC_DEV - 1).astype(jnp.int32)
    return {"psi": psi, "left_env": left_env, "right_env": right_env, "left_pick": left_pick, "right_owner": right_owner, "right_pick": right_pick}


def block_ranks(owners):
    rows = owners.reshape(-1, PAIR_DEV)
    same = rows[:, :, None] == rows[:, None, :]
    idx = jnp.arange(PAIR_DEV)
    earlier = idx[None, :] < idx[:, None]
    return jnp.sum((same & earlier[None]).astype(jnp.int32), axis=2).reshape(-1)


def reference(psi, left_env, right_env, left_pick, right_owner, right_pick):
    source = jnp.arange(PAIRS, dtype=jnp.int32) // PAIR_DEV
    lsec = source * LSEC_DEV + left_pick
    rsec = right_owner * RSEC_DEV + right_pick
    psi_wide = psi.astype(jnp.float32)

    def group(carry, g):
        left_part = lax.dynamic_slice_in_dim(left_env, g * TERM_DEV, TERM_DEV, 0)
        right_part = lax.dynamic_slice_in_dim(right_env, g * TERM_DEV, TERM_DEV, 0)
        left_sel = jnp.take(left_part, lsec, axis=1).astype(jnp.float32)
        right_sel = jnp.take(right_part, rsec, axis=1).astype(jnp.float32)
        half = jnp.einsum('tjab,vjbc->vtjac', left_sel, psi_wide).astype(jnp.bfloat16)
        part = jnp.einsum('vtjab,tjbc->vjac', half.astype(jnp.float32), right_sel).astype(jnp.bfloat16)
        return carry + part.astype(jnp.float32), None

    start = jnp.zeros((VECS, PAIRS, B, B), jnp.float32)
    total, unused = lax.scan(group, start, jnp.arange(N_TERM, dtype=jnp.int32))
    rank = block_ranks(right_owner)
    pos = right_owner * RECV_DEV + source * SLOT + rank
    sigma = jnp.zeros((VECS, RECV_DEV * N_SEC, B, B), jnp.bfloat16)
    return sigma.at[:, pos].set(total.astype(jnp.bfloat16))
```

```python
import jax
import jax.numpy as jnp
from jax import lax
from jax.experimental import pallas as pl
from jax.experimental.pallas import tpu as pltpu
from jax.sharding import PartitionSpec as P

B = 128
VECS = 3
PAIR_DEV = 16
TERM_DEV = 4
NX = 4
NY = 8
NZ = 8
HALF_Y = NY // 2
ENV_ROWS = TERM_DEV * 2 * B
PICK_ROWS = 16
ROWS = 8

X_GROUPS = [[y * NX + x for x in range(NX)] for y in range(NY)]
Y_GROUPS = [[y * NX + x for y in range(NY)] for x in range(NX)]
YZ_GROUPS = [
    [(y * NX + x) * 2 * NZ + z * 2 + c for y in range(NY) for z in range(NZ)]
    for x in range(NX)
    for c in range(2)
]
CORE_SWAP = [(z * 2 + c, z * 2 + 1 - c) for z in range(NZ) for c in range(2)]


def pack_kernel(where_ref, owner_ref, pick_ref, psi_ref, left_ref, psi_out, left_out, table, tile, sems):
    here, core = where_ref[0], where_ref[1]

    def clear(i, _):
        table[i] = 0
        return 0

    lax.fori_loop(0, NX * NY, clear, 0)

    def fill(j, _):
        table[owner_ref[here * PAIR_DEV + j]] = j
        return 0

    lax.fori_loop(0, PAIR_DEV, fill, 0)
    copies = []
    for x in range(NX):
        for i in range(HALF_Y):
            src = table[(core * HALF_Y + i) * NX + x]
            copies.append(
                pltpu.make_async_copy(psi_ref.at[:, src], psi_out.at[x, i], sems.at[x * HALF_Y + i])
            )
    for x in range(NX):
        copies.append(
            pltpu.make_async_copy(
                left_ref, left_out.at[x, pl.ds(0, ENV_ROWS)], sems.at[NX * HALF_Y + x]
            )
        )
    for copy in copies:
        copy.start()
    row = lax.broadcasted_iota(jnp.int32, (PICK_ROWS, B), 0)
    for x in range(NX):
        value = jnp.zeros((PICK_ROWS, B), jnp.int32)
        for y in range(NY):
            value = jnp.where(row == y, pick_ref[table[y * NX + x]], value)
        tile[x] = value.astype(jnp.float32).astype(jnp.bfloat16)
    last = pltpu.make_async_copy(
        tile, left_out.at[:, pl.ds(ENV_ROWS, PICK_ROWS)], sems.at[NX * HALF_Y + NX]
    )
    last.start()
    for copy in copies:
        copy.wait()
    last.wait()


def pack(where, right_owner, left_pick, psi, left):
    smem = pl.BlockSpec(memory_space=pltpu.SMEM)
    hbm = pl.BlockSpec(memory_space=pl.ANY)
    return pl.pallas_call(
        pack_kernel,
        out_shape=(
            jax.ShapeDtypeStruct((NX, HALF_Y, VECS, B, B), jnp.bfloat16),
            jax.ShapeDtypeStruct((NX, ENV_ROWS + PICK_ROWS, B), jnp.bfloat16),
        ),
        in_specs=[smem, smem, smem, hbm, hbm],
        out_specs=(hbm, hbm),
        scratch_shapes=[
            pltpu.SMEM((NX * NY,), jnp.int32),
            pltpu.VMEM((NX, PICK_ROWS, B), jnp.bfloat16),
            pltpu.SemaphoreType.DMA((NX * HALF_Y + NX + 1,)),
        ],
        name="pack",
    )(where, right_owner, left_pick, psi, left)


def half_kernel(where_ref, own_ref, other_ref, left_ref, half_ref):
    group, i = pl.program_id(0), pl.program_id(1)
    right_y = ((group + where_ref[1]) % 2) * HALF_Y + i

    def work(psi_ref):
        for x in range(NX):
            picks = left_ref[x, pl.ds(ENV_ROWS, PICK_ROWS), :].astype(jnp.float32)
            row = lax.broadcasted_iota(jnp.int32, (PICK_ROWS, B), 0)
            second = jnp.max(jnp.where(row == right_y, picks, 0.0), axis=0, keepdims=True) > 0.5
            second = jnp.broadcast_to(second, (B, B))
            lefts = []
            for t in range(TERM_DEV):
                first_env = left_ref[x, pl.ds((t * 2) * B, B), :]
                second_env = left_ref[x, pl.ds((t * 2 + 1) * B, B), :]
                lefts.append(jnp.where(second, second_env, first_env))
            lefts = jnp.concatenate(lefts, axis=0)
            vecs = jnp.concatenate([psi_ref[x, 0, v] for v in range(VECS)], axis=1)
            prod = jnp.dot(lefts, vecs, preferred_element_type=jnp.float32).astype(jnp.bfloat16)
            for t in range(TERM_DEV):
                for v in range(VECS):
                    half_ref[0, x, pl.ds(v * B, B), pl.ds(t * B, B)] = prod[
                        t * B : (t + 1) * B, v * B : (v + 1) * B
                    ]

    @pl.when(group == 0)
    def _():
        work(own_ref)

    @pl.when(group == 1)
    def _():
        work(other_ref)


def half_products(where, own, other, left):
    def psi_block(keep):
        return pl.BlockSpec(
            (NX, 1, VECS, B, B),
            lambda g, i, where_ref: (0, jnp.where(g == keep, i, (HALF_Y - 1) * (1 - keep)), 0, 0, 0),
        )

    return pl.pallas_call(
        half_kernel,
        out_shape=jax.ShapeDtypeStruct((NY, NX, VECS * B, TERM_DEV * B), jnp.bfloat16),
        grid_spec=pltpu.PrefetchScalarGridSpec(
            num_scalar_prefetch=1,
            grid=(2, HALF_Y),
            in_specs=[
                psi_block(0),
                psi_block(1),
                pl.BlockSpec((NX, ENV_ROWS + PICK_ROWS, B), lambda g, i, where_ref: (0, 0, 0)),
            ],
            out_specs=pl.BlockSpec(
                (1, NX, VECS * B, TERM_DEV * B),
                lambda g, i, where_ref: (((g + where_ref[1]) % 2) * HALF_Y + i, 0, 0, 0),
            ),
        ),
        compiler_params=pltpu.CompilerParams(vmem_limit_bytes=32 * 1024 * 1024),
        cost_estimate=pl.CostEstimate(
            flops=2 * NY * NX * VECS * TERM_DEV * B**3, bytes_accessed=17 * 2**20, transcendentals=0
        ),
        name="half",
    )(where, own, other, left)


def part_kernel(where_ref, owner_ref, pick_ref, half_ref, right_ref, keep_ref, give_ref, table):
    right_y = pl.program_id(0)
    here, core = where_ref[0], where_ref[1]
    my_y, my_x = here // NX, here % NX

    @pl.when(right_y == 0)
    def _():
        def clear(i, _):
            table[i] = 0
            return 0

        lax.fori_loop(0, NX * NY, clear, 0)

        def fill(j, _):
            block = my_y * NX * PAIR_DEV + j
            owner = owner_ref[block]
            slot = jnp.where(owner % NX == my_x, (j // PAIR_DEV) * NY + owner // NX, NX * NY)
            table[slot] = pick_ref[block]
            return 0

        lax.fori_loop(0, NX * PAIR_DEV, fill, 0)

    groups = [[[] for _ in range(NZ)] for _ in range(2)]
    for x in range(NX):
        pick = table[x * NY + right_y]
        rights = jnp.concatenate([right_ref[0, t * 2 + pick] for t in range(TERM_DEV)], axis=0)
        prod = jnp.dot(half_ref[0, x], rights, preferred_element_type=jnp.float32)
        for v in range(VECS):
            for z in range(NZ):
                for c in range(2):
                    at = v * B + (z * 2 + c) * ROWS
                    groups[c][z].append(prod[at : at + ROWS])
    packed = [
        [jnp.concatenate(groups[c][z], axis=0).astype(jnp.bfloat16) for z in range(NZ)] for c in range(2)
    ]

    @pl.when(core == 0)
    def _():
        for z in range(NZ):
            keep_ref[0, z] = packed[0][z]
            give_ref[0, z] = packed[1][z]

    @pl.when(core == 1)
    def _():
        for z in range(NZ):
            keep_ref[0, z] = packed[1][z]
            give_ref[0, z] = packed[0][z]


def part_products(where, right_owner, right_pick, half, right):
    out = jax.ShapeDtypeStruct((NY, NZ, NX * VECS * ROWS, B), jnp.bfloat16)
    smem = pl.BlockSpec(memory_space=pltpu.SMEM)
    out_block = pl.BlockSpec((1, NZ, NX * VECS * ROWS, B), lambda y: (y, 0, 0, 0))
    return pl.pallas_call(
        part_kernel,
        out_shape=(out, out),
        grid=(NY,),
        in_specs=[
            smem,
            smem,
            smem,
            pl.BlockSpec((1, NX, VECS * B, TERM_DEV * B), lambda y: (y, 0, 0, 0)),
            pl.BlockSpec((1, TERM_DEV * 2, B, B), lambda y: (y, 0, 0, 0)),
        ],
        out_specs=(out_block, out_block),
        scratch_shapes=[pltpu.SMEM((NX * NY + 1,), jnp.int32)],
        compiler_params=pltpu.CompilerParams(vmem_limit_bytes=32 * 1024 * 1024),
        cost_estimate=pl.CostEstimate(
            flops=2 * NY * NX * VECS * TERM_DEV * B**3, bytes_accessed=18 * 2**20, transcendentals=0
        ),
        name="part",
    )(where, right_owner, right_pick, half, right)


def shards(psi, left_env, right_env, left_pick, right_owner, right_pick):
    here = lax.axis_index("sec")
    where = jnp.stack([here, lax.axis_index("term") % 2]).astype(jnp.int32)
    rights = lax.all_gather(
        right_env.reshape(TERM_DEV * 2, B, B), "sec", axis=0, tiled=False, axis_index_groups=Y_GROUPS
    )
    psi_out, left_out = pack(where, right_owner, left_pick, psi, left_env.reshape(ENV_ROWS, B))
    own = lax.all_to_all(psi_out, "sec", 0, 0, tiled=True, axis_index_groups=X_GROUPS)
    other = lax.ppermute(own, "term", CORE_SWAP)
    left_out, own = lax.optimization_barrier((left_out, own))
    lefts = lax.all_to_all(left_out, "sec", 0, 0, tiled=True, axis_index_groups=X_GROUPS)
    half = half_products(where, own, other, lefts)
    keep, give = part_products(where, right_owner, right_pick, half, rights)
    got = lax.ppermute(give, "term", CORE_SWAP)
    both = (keep.astype(jnp.float32) + got.astype(jnp.float32)).astype(jnp.bfloat16)
    both = both.reshape(NY * NZ, NX * VECS * ROWS, B)
    arrived = lax.all_to_all(both, ("sec", "term"), 0, 0, tiled=True, axis_index_groups=YZ_GROUPS)
    arrived = arrived.reshape(NY, NZ, NX, VECS, ROWS, B)
    total = jnp.sum(arrived.astype(jnp.float32), axis=1)
    total = total.transpose(2, 0, 1, 3, 4).reshape(VECS, NY * NX, ROWS, B)
    valid = jnp.any(right_owner.reshape(-1, PAIR_DEV) == here, axis=1)
    return jnp.where(valid[None, :, None, None], total, 0.0).astype(jnp.bfloat16)


def solution(mesh):
    return jax.shard_map(
        shards,
        mesh=mesh,
        in_specs=(
            P(None, "sec", None, None),
            P("term", "sec", None, None),
            P("term", "sec", None, None),
            P("sec"),
            P(),
            P(),
        ),
        out_specs=P(None, "sec", "term", None),
        check_vma=False,
    )
```

```python
import jax
import jax.numpy as jnp
from jax import lax
from jax.experimental import pallas as pl
from jax.experimental.pallas import tpu as pltpu
from jax.sharding import PartitionSpec as P

B = 128
VECS = 3
PAIR_DEV = 16
TERM_DEV = 4
NX = 4
NY = 8
NZ = 8
HALF_Y = NY // 2
ENV_ROWS = TERM_DEV * 2 * B
PICK_ROWS = 16
PSI_ROWS = HALF_Y * VECS * B
SENT_ROWS = PSI_ROWS + ENV_ROWS + PICK_ROWS
ROWS = 8

X_GROUPS = [[y * NX + x for x in range(NX)] for y in range(NY)]
Y_GROUPS = [[y * NX + x for y in range(NY)] for x in range(NX)]
YZ_GROUPS = [
    [(y * NX + x) * 2 * NZ + z * 2 + c for y in range(NY) for z in range(NZ)]
    for x in range(NX)
    for c in range(2)
]
CORE_SWAP = [(z * 2 + c, z * 2 + 1 - c) for z in range(NZ) for c in range(2)]


def pack_kernel(where_ref, owner_ref, pick_ref, psi_ref, left_ref, out_ref, table, sems):
    here, core = where_ref[0], where_ref[1]

    def clear(i, _):
        table[i] = 0
        return 0

    lax.fori_loop(0, NX * NY, clear, 0)

    def fill(j, _):
        table[owner_ref[here * PAIR_DEV + j]] = j
        return 0

    lax.fori_loop(0, PAIR_DEV, fill, 0)
    copies = []
    for x in range(NX):
        for i in range(HALF_Y):
            src = table[(core * HALF_Y + i) * NX + x]
            for v in range(VECS):
                copies.append(
                    pltpu.make_async_copy(
                        psi_ref.at[v, src],
                        out_ref.at[x, pl.ds((i * VECS + v) * B, B)],
                        sems.at[len(copies)],
                    )
                )
        copies.append(
            pltpu.make_async_copy(
                left_ref, out_ref.at[x, pl.ds(PSI_ROWS, ENV_ROWS)], sems.at[len(copies)]
            )
        )
    for copy in copies:
        copy.start()
    row = lax.broadcasted_iota(jnp.int32, (PICK_ROWS, B), 0)
    for x in range(NX):
        value = jnp.zeros((PICK_ROWS, B), jnp.int32)
        for y in range(NY):
            value = jnp.where(row == y, pick_ref[table[y * NX + x]], value)
        out_ref[x, pl.ds(PSI_ROWS + ENV_ROWS, PICK_ROWS)] = value.astype(jnp.float32).astype(jnp.bfloat16)
    for copy in copies:
        copy.wait()


def pack(where, right_owner, left_pick, psi, left):
    smem = pl.BlockSpec(memory_space=pltpu.SMEM)
    hbm = pl.BlockSpec(memory_space=pl.ANY)
    return pl.pallas_call(
        pack_kernel,
        out_shape=jax.ShapeDtypeStruct((NX, SENT_ROWS, B), jnp.bfloat16),
        in_specs=[smem, smem, smem, hbm, hbm],
        out_specs=pl.BlockSpec(memory_space=pltpu.VMEM),
        scratch_shapes=[
            pltpu.SMEM((NX * NY,), jnp.int32),
            pltpu.SemaphoreType.DMA((NX * (HALF_Y * VECS + 1),)),
        ],
        compiler_params=pltpu.CompilerParams(vmem_limit_bytes=32 * 1024 * 1024),
        name="pack",
    )(where, right_owner, left_pick, psi, left)


def part_kernel(
    where_ref, owner_ref, pick_ref, got_ref, other_ref, right_ref, keep_ref, give_ref, table
):
    group, i = pl.program_id(0), pl.program_id(1)
    here, core = where_ref[0], where_ref[1]
    my_y, my_x = here // NX, here % NX
    right_y = ((group + core) % 2) * HALF_Y + i

    @pl.when((group == 0) & (i == 0))
    def _():
        def clear(k, _):
            table[k] = 0
            return 0

        lax.fori_loop(0, NX * NY, clear, 0)

        def fill(j, _):
            block = my_y * NX * PAIR_DEV + j
            owner = owner_ref[block]
            slot = jnp.where(owner % NX == my_x, (j // PAIR_DEV) * NY + owner // NX, NX * NY)
            table[slot] = pick_ref[block]
            return 0

        lax.fori_loop(0, NX * PAIR_DEV, fill, 0)

    def work(load_psi):
        row = lax.broadcasted_iota(jnp.int32, (PICK_ROWS, B), 0)
        groups = [[[] for _ in range(NZ)] for _ in range(2)]
        for x in range(NX):
            picks = got_ref[x, pl.ds(PSI_ROWS + ENV_ROWS, PICK_ROWS), :].astype(jnp.float32)
            second = jnp.max(jnp.where(row == right_y, picks, 0.0), axis=0, keepdims=True) > 0.5
            second = jnp.broadcast_to(second, (B, B))
            lefts = []
            for t in range(TERM_DEV):
                first_env = got_ref[x, pl.ds(PSI_ROWS + (t * 2) * B, B), :]
                second_env = got_ref[x, pl.ds(PSI_ROWS + (t * 2 + 1) * B, B), :]
                lefts.append(jnp.where(second, second_env, first_env))
            lefts = jnp.concatenate(lefts, axis=0)
            vecs = jnp.concatenate([load_psi(x, v) for v in range(VECS)], axis=1)
            half = jnp.dot(lefts, vecs, preferred_element_type=jnp.float32).astype(jnp.bfloat16)
            half = jnp.concatenate(
                [
                    jnp.concatenate(
                        [half[t * B : (t + 1) * B, v * B : (v + 1) * B] for t in range(TERM_DEV)], axis=1
                    )
                    for v in range(VECS)
                ],
                axis=0,
            )
            pick = table[x * NY + right_y]
            rights = jnp.concatenate([right_ref[0, t * 2 + pick] for t in range(TERM_DEV)], axis=0)
            prod = jnp.dot(half, rights, preferred_element_type=jnp.float32)
            for v in range(VECS):
                for z in range(NZ):
                    for c in range(2):
                        at = v * B + (z * 2 + c) * ROWS
                        groups[c][z].append(prod[at : at + ROWS])
        packed = [
            [jnp.concatenate(groups[c][z], axis=0).astype(jnp.bfloat16) for z in range(NZ)]
            for c in range(2)
        ]

        @pl.when(core == 0)
        def _():
            for z in range(NZ):
                keep_ref[0, z] = packed[0][z]
                give_ref[0, z] = packed[1][z]

        @pl.when(core == 1)
        def _():
            for z in range(NZ):
                keep_ref[0, z] = packed[1][z]
                give_ref[0, z] = packed[0][z]

    @pl.when(group == 0)
    def _():
        work(lambda x, v: got_ref[x, pl.ds(pl.multiple_of(i * VECS * B, B) + v * B, B), :])

    @pl.when(group == 1)
    def _():
        work(lambda x, v: other_ref[x, pl.ds(v * B, B), :])


def part_products(where, right_owner, right_pick, got, other, right):
    out = jax.ShapeDtypeStruct((NY, NZ, NX * VECS * ROWS, B), jnp.bfloat16)
    smem = pl.BlockSpec(memory_space=pltpu.SMEM)

    def right_y(g, i, where_ref):
        return ((g + where_ref[1]) % 2) * HALF_Y + i

    out_block = pl.BlockSpec(
        (1, NZ, NX * VECS * ROWS, B), lambda g, i, where_ref: (right_y(g, i, where_ref), 0, 0, 0)
    )
    return pl.pallas_call(
        part_kernel,
        out_shape=(out, out),
        grid_spec=pltpu.PrefetchScalarGridSpec(
            num_scalar_prefetch=1,
            grid=(2, HALF_Y),
            in_specs=[
                smem,
                smem,
                pl.BlockSpec((NX, SENT_ROWS, B), lambda g, i, where_ref: (0, 0, 0)),
                pl.BlockSpec((NX, VECS * B, B), lambda g, i, where_ref: (0, g * i, 0)),
                pl.BlockSpec(
                    (1, TERM_DEV * 2, B, B),
                    lambda g, i, where_ref: (right_y(g, i, where_ref), 0, 0, 0),
                ),
            ],
            out_specs=(out_block, out_block),
            scratch_shapes=[pltpu.SMEM((NX * NY + 1,), jnp.int32)],
        ),
        compiler_params=pltpu.CompilerParams(vmem_limit_bytes=32 * 1024 * 1024),
        cost_estimate=pl.CostEstimate(
            flops=4 * NY * NX * VECS * TERM_DEV * B**3, bytes_accessed=10 * 2**20, transcendentals=0
        ),
        name="part",
    )(where, right_owner, right_pick, got, other, right)


def shards(psi, left_env, right_env, left_pick, right_owner, right_pick):
    here = lax.axis_index("sec")
    where = jnp.stack([here, lax.axis_index("term") % 2]).astype(jnp.int32)
    rights = lax.all_gather(
        right_env.reshape(TERM_DEV * 2, B, B), "sec", axis=0, tiled=False, axis_index_groups=Y_GROUPS
    )
    valid = jnp.any(right_owner.reshape(-1, PAIR_DEV) == here, axis=1)
    sent = pack(where, right_owner, left_pick, psi, left_env.reshape(ENV_ROWS, B))
    got = lax.all_to_all(sent, "sec", 0, 0, tiled=True, axis_index_groups=X_GROUPS)
    other = lax.ppermute(got[:, :PSI_ROWS], "term", CORE_SWAP)
    keep, give = part_products(where, right_owner, right_pick, got, other, rights)
    taken = lax.ppermute(give, "term", CORE_SWAP)
    both = (keep.astype(jnp.float32) + taken.astype(jnp.float32)).astype(jnp.bfloat16)
    both = both.reshape(NY * NZ, NX * VECS * ROWS, B)
    both, valid = lax.optimization_barrier((both, valid))
    arrived = lax.all_to_all(both, ("sec", "term"), 0, 0, tiled=True, axis_index_groups=YZ_GROUPS)
    arrived = arrived.reshape(NY, NZ, NX, VECS, ROWS, B)
    total = jnp.sum(arrived.astype(jnp.float32), axis=1)
    total = total.transpose(2, 0, 1, 3, 4).reshape(VECS, NY * NX, ROWS, B)
    return jnp.where(valid[None, :, None, None], total, 0.0).astype(jnp.bfloat16)


def solution(mesh):
    return jax.shard_map(
        shards,
        mesh=mesh,
        in_specs=(
            P(None, "sec", None, None),
            P("term", "sec", None, None),
            P("term", "sec", None, None),
            P("sec"),
            P(),
            P(),
        ),
        out_specs=P(None, "sec", "term", None),
        check_vma=False,
    )
```

```python
import jax
import jax.numpy as jnp
from jax import lax
from jax.experimental import pallas as pl
from jax.experimental.pallas import tpu as pltpu
from jax.sharding import PartitionSpec as P

B = 128
VECS = 3
PAIR_DEV = 16
TERM_DEV = 4
NX = 4
NY = 8
NZ = 8
HALF_Y = NY // 2
ENV_ROWS = TERM_DEV * 2 * B
PICK_ROWS = 16
PSI_ROWS = HALF_Y * VECS * B
SENT_ROWS = PSI_ROWS + ENV_ROWS + PICK_ROWS
ROWS = 8

X_GROUPS = [[y * NX + x for x in range(NX)] for y in range(NY)]
Y_GROUPS = [[y * NX + x for y in range(NY)] for x in range(NX)]
YZ_GROUPS = [
    [((y + c * HALF_Y) % NY * NX + x) * 2 * NZ + z * 2 + c for y in range(NY) for z in range(NZ)]
    for x in range(NX)
    for c in range(2)
]
CORE_SWAP = [(z * 2 + c, z * 2 + 1 - c) for z in range(NZ) for c in range(2)]


def pack_kernel(where_ref, owner_ref, pick_ref, psi_ref, left_ref, out_ref, table, sems):
    here, core = where_ref[0], where_ref[1]

    def clear(i, _):
        table[i] = 0
        return 0

    lax.fori_loop(0, NX * NY, clear, 0)

    def fill(j, _):
        table[owner_ref[here * PAIR_DEV + j]] = j
        return 0

    lax.fori_loop(0, PAIR_DEV, fill, 0)
    copies = []
    for x in range(NX):
        for i in range(HALF_Y):
            src = table[(core * HALF_Y + i) * NX + x]
            for v in range(VECS):
                copies.append(
                    pltpu.make_async_copy(
                        psi_ref.at[v, src],
                        out_ref.at[x, pl.ds((i * VECS + v) * B, B)],
                        sems.at[len(copies)],
                    )
                )
        copies.append(
            pltpu.make_async_copy(
                left_ref, out_ref.at[x, pl.ds(PSI_ROWS, ENV_ROWS)], sems.at[len(copies)]
            )
        )
    for copy in copies:
        copy.start()
    row = lax.broadcasted_iota(jnp.int32, (PICK_ROWS, B), 0)
    for x in range(NX):
        value = jnp.zeros((PICK_ROWS, B), jnp.int32)
        for y in range(NY):
            value = jnp.where(row == y, pick_ref[table[y * NX + x]], value)
        out_ref[x, pl.ds(PSI_ROWS + ENV_ROWS, PICK_ROWS)] = value.astype(jnp.float32).astype(jnp.bfloat16)
    for copy in copies:
        copy.wait()


def pack(where, right_owner, left_pick, psi, left):
    smem = pl.BlockSpec(memory_space=pltpu.SMEM)
    hbm = pl.BlockSpec(memory_space=pl.ANY)
    return pl.pallas_call(
        pack_kernel,
        out_shape=jax.ShapeDtypeStruct((NX, SENT_ROWS, B), jnp.bfloat16),
        in_specs=[smem, smem, smem, hbm, hbm],
        out_specs=pl.BlockSpec(memory_space=pltpu.VMEM),
        scratch_shapes=[
            pltpu.SMEM((NX * NY,), jnp.int32),
            pltpu.SemaphoreType.DMA((NX * (HALF_Y * VECS + 1),)),
        ],
        name="pack",
    )(where, right_owner, left_pick, psi, left)


def part_kernel(mine, where_ref, owner_ref, pick_ref, got_ref, psi_ref, right_ref, keep_ref, give_ref, table, rows):
    i = pl.program_id(0)
    core = where_ref[1]
    right_y = (core if mine else 1 - core) * HALF_Y + i

    @pl.when(i == 0)
    def _():
        here = where_ref[0]
        my_x = here & (NX - 1)
        first = (here - my_x) * PAIR_DEV

        for k in range(NX * NY):
            table[k] = 0

        def fill(j, _):
            owner = owner_ref[first + j]
            slot = lax.shift_right_logical(j, 4) * NY + lax.shift_right_logical(owner, 2)
            table[jnp.where((owner & (NX - 1)) == my_x, slot, NX * NY)] = pick_ref[first + j]
            return 0

        lax.fori_loop(0, NX * PAIR_DEV, fill, 0, unroll=8)

    row = lax.broadcasted_iota(jnp.int32, (PICK_ROWS, B), 0)
    groups = [[[] for _ in range(NZ)] for _ in range(2)]
    for x in range(NX):
        picks = got_ref[x, pl.ds(PSI_ROWS + ENV_ROWS, PICK_ROWS), :].astype(jnp.float32)
        second = jnp.max(jnp.where(row == right_y, picks, 0.0), axis=0, keepdims=True) > 0.5
        second = jnp.broadcast_to(second, (B, B))
        lefts = []
        for t in range(TERM_DEV):
            first_env = got_ref[x, pl.ds(PSI_ROWS + (t * 2) * B, B), :]
            second_env = got_ref[x, pl.ds(PSI_ROWS + (t * 2 + 1) * B, B), :]
            lefts.append(jnp.where(second, second_env, first_env))
        lefts = jnp.concatenate(lefts, axis=0)
        pick = table[x * NY + right_y]
        rights = jnp.concatenate([right_ref[0, t * 2 + pick] for t in range(TERM_DEV)], axis=0)
        for v in range(VECS):
            if mine:
                vec = psi_ref[x, pl.ds(pl.multiple_of(i * VECS * B, B) + v * B, B), :]
            else:
                vec = psi_ref[x, pl.ds(v * B, B), :]
            half = jnp.dot(lefts, vec, preferred_element_type=jnp.float32).astype(jnp.bfloat16)
            half = jnp.concatenate([half[t * B : (t + 1) * B] for t in range(TERM_DEV)], axis=1)
            prod = jnp.dot(half, rights, preferred_element_type=jnp.float32)
            for z in range(NZ):
                for c in range(2):
                    at = (z * 2 + c) * ROWS
                    groups[c][z].append(prod[at : at + ROWS])
    for c in range(2):
        for z in range(NZ):
            rows[core ^ c, z] = jnp.concatenate(groups[c][z], axis=0).astype(jnp.bfloat16)
    keep_ref[0] = rows[0]
    give_ref[0] = rows[1]


def part_products(mine, where, right_owner, right_pick, got, psi, right):
    out = jax.ShapeDtypeStruct((HALF_Y, NZ, NX * VECS * ROWS, B), jnp.bfloat16)
    smem = pl.BlockSpec(memory_space=pltpu.SMEM)
    got_block = pl.BlockSpec((NX, SENT_ROWS, B), lambda i, where_ref: (0, 0, 0))
    psi_block = pl.BlockSpec((NX, VECS * B, B), lambda i, where_ref: (0, i, 0))
    out_block = pl.BlockSpec((1, NZ, NX * VECS * ROWS, B), lambda i, where_ref: (i, 0, 0, 0))

    def right_y(i, where_ref):
        return (where_ref[1] if mine else 1 - where_ref[1]) * HALF_Y + i

    def kernel(where_ref, owner_ref, pick_ref, got_ref, *rest):
        if mine:
            rest = (got_ref, *rest)
        part_kernel(mine, where_ref, owner_ref, pick_ref, got_ref, *rest)

    return pl.pallas_call(
        kernel,
        out_shape=(out, out),
        grid_spec=pltpu.PrefetchScalarGridSpec(
            num_scalar_prefetch=1,
            grid=(HALF_Y,),
            in_specs=[smem, smem, got_block]
            + ([] if mine else [psi_block])
            + [
                pl.BlockSpec(
                    (1, TERM_DEV * 2, B, B), lambda i, where_ref: (right_y(i, where_ref), 0, 0, 0)
                )
            ],
            out_specs=(out_block, out_block),
            scratch_shapes=[
                pltpu.SMEM((NX * NY + 1,), jnp.int32),
                pltpu.VMEM((2, NZ, NX * VECS * ROWS, B), jnp.bfloat16),
            ],
        ),
        cost_estimate=pl.CostEstimate(
            flops=2 * NY * NX * VECS * TERM_DEV * B**3, bytes_accessed=6 * 2**20, transcendentals=0
        ),
        name="part_own" if mine else "part_other",
    )(where, right_owner, right_pick, got, *(() if mine else (psi,)), right)


def add_kernel(keep_a, taken_a, keep_b, taken_b, out_ref):
    out_ref[0] = (keep_a[...].astype(jnp.float32) + taken_a[...].astype(jnp.float32)).astype(jnp.bfloat16)
    out_ref[1] = (keep_b[...].astype(jnp.float32) + taken_b[...].astype(jnp.float32)).astype(jnp.bfloat16)


def add_rows(keep_a, taken_a, keep_b, taken_b):
    block = (1,) + keep_a.shape[1:]
    return pl.pallas_call(
        add_kernel,
        out_shape=jax.ShapeDtypeStruct((2,) + keep_a.shape, jnp.bfloat16),
        grid=(HALF_Y,),
        in_specs=[pl.BlockSpec(block, lambda i: (i, 0, 0, 0))] * 4,
        out_specs=pl.BlockSpec((2,) + block, lambda i: (0, i, 0, 0, 0)),
        name="add_rows",
    )(keep_a, taken_a, keep_b, taken_b)


def sum_kernel(where_ref, valid_ref, arrived_ref, out_ref):
    first = ((pl.program_id(0) + where_ref[1]) & 1) * HALF_Y * NX
    for y in range(HALF_Y):
        total = arrived_ref[y, 0].astype(jnp.float32)
        for z in range(1, NZ):
            total = total + arrived_ref[y, z].astype(jnp.float32)
        for v in range(VECS):
            blocks = []
            for x in range(NX):
                block = total[(x * VECS + v) * ROWS : (x * VECS + v + 1) * ROWS]
                blocks.append(jnp.where(valid_ref[first + y * NX + x] > 0, block, 0.0))
            out_ref[v, pl.ds(y * NX * ROWS, NX * ROWS)] = jnp.concatenate(blocks, axis=0).astype(jnp.bfloat16)


def sum_rows(where, valid, arrived):
    return pl.pallas_call(
        sum_kernel,
        out_shape=jax.ShapeDtypeStruct((VECS, NY * NX * ROWS, B), jnp.bfloat16),
        grid_spec=pltpu.PrefetchScalarGridSpec(
            num_scalar_prefetch=1,
            grid=(2,),
            in_specs=[
                pl.BlockSpec(memory_space=pltpu.SMEM),
                pl.BlockSpec((HALF_Y,) + arrived.shape[1:], lambda i, where_ref: (i, 0, 0, 0)),
            ],
            out_specs=pl.BlockSpec(
                (VECS, HALF_Y * NX * ROWS, B), lambda i, where_ref: (0, (i + where_ref[1]) & 1, 0)
            ),
        ),
        name="sum_rows",
    )(where, valid, arrived)


def shards(psi, left_env, right_env, left_pick, right_owner, right_pick):
    here = lax.axis_index("sec")
    where = jnp.stack([here, lax.axis_index("term") % 2]).astype(jnp.int32)
    rights = lax.all_gather(
        right_env.reshape(TERM_DEV * 2, B, B), "sec", axis=0, tiled=False, axis_index_groups=Y_GROUPS
    )
    valid = jnp.any(right_owner.reshape(-1, PAIR_DEV) == here, axis=1).astype(jnp.int32)
    sent = pack(where, right_owner, left_pick, psi, left_env.reshape(ENV_ROWS, B))
    got = lax.all_to_all(sent, "sec", 0, 0, tiled=True, axis_index_groups=X_GROUPS)
    other = lax.ppermute(got[:, :PSI_ROWS], "term", CORE_SWAP)
    part = (where, right_owner, right_pick, got)
    keep_own, give_own = part_products(True, *part, None, rights)
    taken_other = lax.ppermute(give_own, "term", CORE_SWAP)
    other, keep_own = lax.optimization_barrier((other, keep_own))
    keep_other, give_other = part_products(False, *part, other, rights)
    taken_own = lax.ppermute(give_other, "term", CORE_SWAP)
    both = add_rows(keep_own, taken_own, keep_other, taken_other)
    both = both.reshape(NY * NZ, NX * VECS * ROWS, B)
    both, valid = lax.optimization_barrier((both, valid))
    arrived = lax.all_to_all(both, ("sec", "term"), 0, 0, tiled=True, axis_index_groups=YZ_GROUPS)
    total = sum_rows(where, valid, arrived.reshape(NY, NZ, NX * VECS * ROWS, B))
    return total.reshape(VECS, NY * NX, ROWS, B)


def solution(mesh):
    return jax.shard_map(
        shards,
        mesh=mesh,
        in_specs=(
            P(None, "sec", None, None),
            P("term", "sec", None, None),
            P("term", "sec", None, None),
            P("sec"),
            P(),
            P(),
        ),
        out_specs=P(None, "sec", "term", None),
        check_vma=False,
    )
```

```python
import jax
import jax.numpy as jnp
from jax import lax
from jax.experimental import pallas as pl
from jax.experimental.pallas import tpu as pltpu
from jax.sharding import PartitionSpec as P

B = 128
VECS = 3
PAIR_DEV = 16
TERM_DEV = 4
NX = 4
NY = 8
NZ = 8
HALF_Y = NY // 2
ROWS = 8
CORE_ROWS = B // 2
ENVS = TERM_DEV * 2
PSI_ROWS = HALF_Y * VECS * B
ENV_ROWS = ENVS * CORE_ROWS
PICK_ROWS = 16
SWAP_ROWS = PSI_ROWS + ENV_ROWS
SENT_ROWS = SWAP_ROWS + ENV_ROWS + PICK_ROWS
OUT_ROWS = NX * VECS * ROWS

X_GROUPS = [[y * NX + x for x in range(NX)] for y in range(NY)]
YC_GROUPS = [
    [(y * NX + x) * 2 * NZ + z * 2 + c for y in range(NY) for c in range(2)]
    for x in range(NX)
    for z in range(NZ)
]
YZ_GROUPS = [
    [(y * NX + x) * 2 * NZ + z * 2 + c for y in range(NY) for z in range(NZ)]
    for x in range(NX)
    for c in range(2)
]
CORE_SWAP = [(z * 2 + c, z * 2 + 1 - c) for z in range(NZ) for c in range(2)]


def core_rows(block, c):
    wide = block.astype(jnp.float32)
    parts = [wide[(z * 2 + c) * ROWS : (z * 2 + c + 1) * ROWS] for z in range(NZ)]
    return jnp.concatenate(parts, axis=0).astype(jnp.bfloat16)


def pack_kernel(
    psi_ref,
    left_hbm,
    owner_hbm,
    lpick_hbm,
    rpick_hbm,
    out_ref,
    slot_ref,
    left,
    owner,
    lpick,
    rpick,
    table,
    sems,
    load_sems,
):
    here = lax.axis_index("sec")
    core = lax.axis_index("term") & 1
    loads = [
        pltpu.make_async_copy(owner_hbm, owner, load_sems.at[0]),
        pltpu.make_async_copy(left_hbm, left, load_sems.at[1]),
        pltpu.make_async_copy(lpick_hbm, lpick, load_sems.at[2]),
        pltpu.make_async_copy(rpick_hbm, rpick, load_sems.at[3]),
    ]
    for load in loads:
        load.start()
    for k in range(NX * NY):
        table[k] = 0
        slot_ref[k] = -1
    loads[0].wait()

    def fill(j, _):
        table[owner[here * PAIR_DEV + j]] = j
        return 0

    lax.fori_loop(0, PAIR_DEV, fill, 0, unroll=True)
    copies = []
    for x in range(NX):
        for i in range(HALF_Y):
            src = table[(core * HALF_Y + i) * NX + x]
            for v in range(VECS):
                copies.append(
                    pltpu.make_async_copy(
                        psi_ref.at[v, src],
                        out_ref.at[x, pl.ds((i * VECS + v) * B, B)],
                        sems.at[len(copies)],
                    )
                )
    for copy in copies:
        copy.start()
    loads[1].wait()
    for k in range(ENVS):
        block = left[k]
        for c in range(2):
            part = core_rows(block, c)
            at = pl.multiple_of(PSI_ROWS + (1 - (core ^ c)) * ENV_ROWS + k * CORE_ROWS, CORE_ROWS)
            for x in range(NX):
                out_ref[x, pl.ds(at, CORE_ROWS)] = part
    for load in loads[2:]:
        load.wait()
    row = lax.broadcasted_iota(jnp.int32, (PICK_ROWS, B), 0)
    for x in range(NX):
        value = jnp.zeros((PICK_ROWS, B), jnp.int32)
        for y in range(NY):
            value = jnp.where(row == y, lpick[table[y * NX + x]], value)
        out_ref[x, pl.ds(SENT_ROWS - PICK_ROWS, PICK_ROWS)] = value.astype(jnp.float32).astype(jnp.bfloat16)
    my_x = here & (NX - 1)
    first = (here - my_x) * PAIR_DEV

    def slots(j, _):
        right = owner[first + j]
        slot = lax.shift_right_logical(j, 4) * NY + lax.shift_right_logical(right, 2)
        slot_ref[jnp.where((right & (NX - 1)) == my_x, slot, NX * NY)] = rpick[first + j]
        return 0

    lax.fori_loop(0, NX * PAIR_DEV, slots, 0, unroll=8)
    for copy in copies:
        copy.wait()


def pack(psi, left, right_owner, left_pick, right_pick):
    hbm = pl.BlockSpec(memory_space=pltpu.HBM)
    return pl.pallas_call(
        pack_kernel,
        out_shape=(
            jax.ShapeDtypeStruct((NX, SENT_ROWS, B), jnp.bfloat16),
            jax.ShapeDtypeStruct((NX * NY + 1,), jnp.int32),
        ),
        in_specs=[hbm] * 5,
        out_specs=(pl.BlockSpec(memory_space=pltpu.VMEM), pl.BlockSpec(memory_space=pltpu.SMEM)),
        scratch_shapes=[
            pltpu.VMEM(left.shape, jnp.bfloat16),
            pltpu.SMEM(right_owner.shape, jnp.int32),
            pltpu.SMEM(left_pick.shape, jnp.int32),
            pltpu.SMEM(right_pick.shape, jnp.int32),
            pltpu.SMEM((NX * NY,), jnp.int32),
            pltpu.SemaphoreType.DMA((NX * HALF_Y * VECS,)),
            pltpu.SemaphoreType.DMA((4,)),
        ],
        compiler_params=pltpu.CompilerParams(vmem_limit_bytes=16 * 1024 * 1024),
        name="pack",
    )(psi, left, right_owner, left_pick, right_pick)


def part_kernel(slot_ref, got_ref, other_ref, right_hbm, out_ref, right, rows, sems):
    core = lax.axis_index("term") & 1

    def order(step):
        return ((core * HALF_Y) + step) & (NY - 1)

    def load(step):
        return pltpu.make_async_copy(
            right_hbm.at[pl.ds(order(step) * 2, 2)], right.at[pl.ds(step * 2, 2)], sems.at[step]
        )

    for step in range(NY):
        load(step).start()
    row = lax.broadcasted_iota(jnp.int32, (PICK_ROWS, B), 0)

    def work(step, psi_ref):
        right_y = order(step)
        load(step).wait()
        for x in range(NX):
            pick = slot_ref[x * NY + right_y]

            @pl.when(pick >= 0)
            def _():
                picks = got_ref[x, pl.ds(SENT_ROWS - PICK_ROWS, PICK_ROWS), :].astype(jnp.float32)
                second = jnp.max(jnp.where(row == right_y, picks, 0.0), axis=0, keepdims=True) > 0.5
                second = jnp.broadcast_to(second, (CORE_ROWS, B))
                lefts = []
                for ref, at in ((got_ref, SWAP_ROWS), (other_ref, PSI_ROWS)):
                    for t in range(TERM_DEV):
                        first_env = ref[x, pl.ds(at + (t * 2) * CORE_ROWS, CORE_ROWS), :]
                        second_env = ref[x, pl.ds(at + (t * 2 + 1) * CORE_ROWS, CORE_ROWS), :]
                        lefts.append(jnp.where(second, second_env, first_env))
                lefts = jnp.concatenate(lefts, axis=0)
                rights = jnp.concatenate(
                    [right[step * 2 + c, t * 2 + pick] for c in (core, 1 - core) for t in range(TERM_DEV)],
                    axis=0,
                )
                at = pl.multiple_of((step & (HALF_Y - 1)) * VECS * B, B)
                halves = []
                for v in range(VECS):
                    vec = psi_ref[x, pl.ds(at + v * B, B), :]
                    half = jnp.dot(lefts, vec, preferred_element_type=jnp.float32).astype(jnp.bfloat16)
                    halves.append(
                        jnp.concatenate(
                            [half[t * CORE_ROWS : (t + 1) * CORE_ROWS] for t in range(2 * TERM_DEV)], axis=1
                        )
                    )
                prod = jnp.dot(jnp.concatenate(halves, axis=0), rights, preferred_element_type=jnp.float32)
                for v in range(VECS):
                    for z in range(NZ):
                        rows[z, pl.ds((x * VECS + v) * ROWS, ROWS)] = prod[
                            v * CORE_ROWS + z * ROWS : v * CORE_ROWS + (z + 1) * ROWS
                        ]

        for z in range(NZ):
            out_ref[right_y, z] = rows[z].astype(jnp.bfloat16)

    rows[...] = jnp.zeros_like(rows)
    pl.loop(0, HALF_Y)(lambda step: work(step, got_ref))
    pl.loop(HALF_Y, NY)(lambda step: work(step, other_ref))


def part_products(slots, got, other, right):
    vmem = pl.BlockSpec(memory_space=pltpu.VMEM)
    return pl.pallas_call(
        part_kernel,
        out_shape=jax.ShapeDtypeStruct((NY, NZ, OUT_ROWS, B), jnp.bfloat16),
        in_specs=[
            pl.BlockSpec(memory_space=pltpu.SMEM),
            vmem,
            vmem,
            pl.BlockSpec(memory_space=pltpu.HBM),
        ],
        out_specs=vmem,
        scratch_shapes=[
            pltpu.VMEM((2 * NY, ENVS, B, B), jnp.bfloat16),
            pltpu.VMEM((NZ, OUT_ROWS, B), jnp.float32),
            pltpu.SemaphoreType.DMA((NY,)),
        ],
        compiler_params=pltpu.CompilerParams(vmem_limit_bytes=20 * 1024 * 1024),
        cost_estimate=pl.CostEstimate(
            flops=4 * NY * NX * VECS * TERM_DEV * B**3, bytes_accessed=10 * 2**20, transcendentals=0
        ),
        name="part",
    )(slots, got, other, right)


def shards(psi, left_env, right_env, left_pick, right_owner, right_pick):
    here = lax.axis_index("sec")
    rights = lax.all_gather(
        right_env.reshape(ENVS, B, B), ("sec", "term"), axis=0, tiled=False, axis_index_groups=YC_GROUPS
    )
    valid = jnp.any(right_owner.reshape(-1, PAIR_DEV) == here, axis=1)
    held = (psi, left_env.reshape(ENVS, B, B), right_owner, left_pick, right_pick)
    sent, slots = pack(*(pltpu.with_memory_space_constraint(a, pltpu.HBM) for a in held))
    got = lax.all_to_all(sent, "sec", 0, 0, tiled=True, axis_index_groups=X_GROUPS)
    other = lax.ppermute(got[:, :SWAP_ROWS], "term", CORE_SWAP)
    rights = pltpu.with_memory_space_constraint(rights, pltpu.HBM)
    both = part_products(slots, got, other, rights).reshape(NY * NZ, OUT_ROWS, B)
    both, valid = lax.optimization_barrier((both, valid))
    arrived = lax.all_to_all(both, ("sec", "term"), 0, 0, tiled=True, axis_index_groups=YZ_GROUPS)
    arrived = arrived.reshape(NY, NZ, NX, VECS, ROWS, B)
    total = jnp.sum(arrived.astype(jnp.float32), axis=1)
    total = total.transpose(2, 0, 1, 3, 4).reshape(VECS, NY * NX, ROWS, B)
    return jnp.where(valid[None, :, None, None], total, 0.0).astype(jnp.bfloat16)


def solution(mesh):
    return jax.shard_map(
        shards,
        mesh=mesh,
        in_specs=(
            P(None, "sec", None, None),
            P("term", "sec", None, None),
            P("term", "sec", None, None),
            P("sec"),
            P(),
            P(),
        ),
        out_specs=P(None, "sec", "term", None),
        check_vma=False,
    )
```

```python
import jax
import jax.numpy as jnp
from jax import lax
from jax.experimental import pallas as pl
from jax.experimental.pallas import tpu as pltpu
from jax.sharding import PartitionSpec as P

B = 128
VECS = 3
PAIR_DEV = 16
TERM_DEV = 4
NX = 4
NY = 8
NZ = 8
HALF_Y = NY // 2
ROWS = 8
CORE_ROWS = B // 2
ENVS = TERM_DEV * 2
PSI_ROWS = HALF_Y * VECS * B
ENV_ROWS = ENVS * CORE_ROWS
PICK_ROWS = 16
SWAP_ROWS = PSI_ROWS + ENV_ROWS
SENT_ROWS = SWAP_ROWS + ENV_ROWS + PICK_ROWS
OUT_ROWS = NX * VECS * ROWS
LIST = NX * HALF_Y + 2

X_GROUPS = [[y * NX + x for x in range(NX)] for y in range(NY)]
YC_GROUPS = [
    [(y * NX + x) * 2 * NZ + z * 2 + c for y in range(NY) for c in range(2)]
    for x in range(NX)
    for z in range(NZ)
]
YZ_GROUPS = [
    [(y * NX + x) * 2 * NZ + z * 2 + c for y in range(NY) for z in range(NZ)]
    for x in range(NX)
    for c in range(2)
]
CORE_SWAP = [(z * 2 + c, z * 2 + 1 - c) for z in range(NZ) for c in range(2)]


def core_rows(block, c):
    wide = block.astype(jnp.float32)
    parts = [wide[(z * 2 + c) * ROWS : (z * 2 + c + 1) * ROWS] for z in range(NZ)]
    return jnp.concatenate(parts, axis=0).astype(jnp.bfloat16)


def pack_kernel(
    psi_ref,
    left_hbm,
    owner_hbm,
    lpick_hbm,
    rpick_hbm,
    out_ref,
    slot_ref,
    left,
    owner,
    lpick,
    rpick,
    table,
    picks,
    sems,
    load_sems,
):
    here = lax.axis_index("sec")
    core = lax.axis_index("term") & 1
    loads = [
        pltpu.make_async_copy(owner_hbm, owner, load_sems.at[0]),
        pltpu.make_async_copy(left_hbm, left, load_sems.at[1]),
        pltpu.make_async_copy(lpick_hbm, lpick, load_sems.at[2]),
        pltpu.make_async_copy(rpick_hbm, rpick, load_sems.at[3]),
    ]
    for load in loads:
        load.start()
    for k in range(NX * NY):
        table[k] = 0
        picks[k] = -1
    loads[0].wait()

    def fill(j, _):
        table[owner[here * PAIR_DEV + j]] = j
        return 0

    lax.fori_loop(0, PAIR_DEV, fill, 0, unroll=True)
    copies = []
    for x in range(NX):
        for i in range(HALF_Y):
            src = table[(core * HALF_Y + i) * NX + x]
            for v in range(VECS):
                copies.append(
                    pltpu.make_async_copy(
                        psi_ref.at[v, src],
                        out_ref.at[x, pl.ds((i * VECS + v) * B, B)],
                        sems.at[len(copies)],
                    )
                )
    for copy in copies:
        copy.start()
    loads[1].wait()
    for k in range(ENVS):
        block = left[k]
        for c in range(2):
            part = core_rows(block, c)
            at = pl.multiple_of(PSI_ROWS + (1 - (core ^ c)) * ENV_ROWS + k * CORE_ROWS, CORE_ROWS)
            for x in range(NX):
                out_ref[x, pl.ds(at, CORE_ROWS)] = part
    for load in loads[2:]:
        load.wait()
    row = lax.broadcasted_iota(jnp.int32, (PICK_ROWS, B), 0)
    for x in range(NX):
        value = jnp.zeros((PICK_ROWS, B), jnp.int32)
        for y in range(NY):
            value = jnp.where(row == y, lpick[table[y * NX + x]], value)
        out_ref[x, pl.ds(SENT_ROWS - PICK_ROWS, PICK_ROWS)] = value.astype(jnp.float32).astype(jnp.bfloat16)
    my_x = here & (NX - 1)
    first = (here - my_x) * PAIR_DEV

    def slots(j, _):
        right = owner[first + j]
        slot = lax.shift_right_logical(j, 4) * NY + lax.shift_right_logical(right, 2)
        picks[jnp.where((right & (NX - 1)) == my_x, slot, NX * NY)] = rpick[first + j]
        return 0

    lax.fori_loop(0, NX * PAIR_DEV, slots, 0, unroll=8)
    for side in range(2):
        base = side * LIST

        def entry(k, count):
            y = (((core + side) & 1) * HALF_Y) + lax.shift_right_logical(k, 2)
            x = k & (NX - 1)
            pick = picks[x * NY + y]
            slot_ref[base + 1 + count] = (k * 2 + pick) & (2 * NX * HALF_Y - 1)
            return count + jnp.where(pick >= 0, 1, 0)

        count = lax.fori_loop(0, NX * HALF_Y, entry, 0, unroll=4)
        slot_ref[base] = lax.shift_right_logical(count + 1, 1)
        slot_ref[base + 1 + count] = slot_ref[base + jnp.maximum(count, 1)]
    for copy in copies:
        copy.wait()


def pack(psi, left, right_owner, left_pick, right_pick):
    hbm = pl.BlockSpec(memory_space=pltpu.HBM)
    return pl.pallas_call(
        pack_kernel,
        out_shape=(
            jax.ShapeDtypeStruct((NX, SENT_ROWS, B), jnp.bfloat16),
            jax.ShapeDtypeStruct((2 * LIST,), jnp.int32),
        ),
        in_specs=[hbm] * 5,
        out_specs=(pl.BlockSpec(memory_space=pltpu.VMEM), pl.BlockSpec(memory_space=pltpu.SMEM)),
        scratch_shapes=[
            pltpu.VMEM(left.shape, jnp.bfloat16),
            pltpu.SMEM(right_owner.shape, jnp.int32),
            pltpu.SMEM(left_pick.shape, jnp.int32),
            pltpu.SMEM(right_pick.shape, jnp.int32),
            pltpu.SMEM((NX * NY,), jnp.int32),
            pltpu.SMEM((NX * NY + 1,), jnp.int32),
            pltpu.SemaphoreType.DMA((NX * HALF_Y * VECS,)),
            pltpu.SemaphoreType.DMA((4,)),
        ],
        compiler_params=pltpu.CompilerParams(vmem_limit_bytes=16 * 1024 * 1024),
        name="pack",
    )(psi, left, right_owner, left_pick, right_pick)


def part_kernel(slot_ref, got_ref, other_ref, right_hbm, out_ref, right, rows, sems):
    core = lax.axis_index("term") & 1

    def load(side):
        return pltpu.make_async_copy(
            right_hbm.at[pl.ds(((core + side) & 1) * 2 * HALF_Y, 2 * HALF_Y)],
            right.at[pl.ds(side * 2 * HALF_Y, 2 * HALF_Y)],
            sems.at[side],
        )

    load(0).start()
    load(1).start()
    rows[...] = jnp.zeros_like(rows)
    row = lax.broadcasted_iota(jnp.int32, (PICK_ROWS, B), 0)

    def product(side, entry):
        psi_ref = (got_ref, other_ref)[side]
        pick, x, i = entry & 1, lax.shift_right_logical(entry, 1) & (NX - 1), lax.shift_right_logical(entry, 3)
        right_y = ((core + side) & 1) * HALF_Y + i
        picks = got_ref[x, pl.ds(SENT_ROWS - PICK_ROWS, PICK_ROWS), :].astype(jnp.float32)
        second = jnp.max(jnp.where(row == right_y, picks, 0.0), axis=0, keepdims=True) > 0.5
        second = jnp.broadcast_to(second, (CORE_ROWS, B))
        lefts = []
        for ref, at in ((got_ref, SWAP_ROWS), (other_ref, PSI_ROWS)):
            for t in range(TERM_DEV):
                first_env = ref[x, pl.ds(at + (t * 2) * CORE_ROWS, CORE_ROWS), :]
                second_env = ref[x, pl.ds(at + (t * 2 + 1) * CORE_ROWS, CORE_ROWS), :]
                lefts.append(jnp.where(second, second_env, first_env))
        lefts = jnp.concatenate(lefts, axis=0)
        at = (side * HALF_Y + i) * 2
        rights = jnp.concatenate(
            [right[at + c, t * 2 + pick] for c in (core, 1 - core) for t in range(TERM_DEV)], axis=0
        )
        halves = []
        for v in range(VECS):
            vec = psi_ref[x, pl.ds(pl.multiple_of((i * VECS + v) * B, B), B), :]
            half = jnp.dot(lefts, vec, preferred_element_type=jnp.float32).astype(jnp.bfloat16)
            halves.append(
                jnp.concatenate(
                    [half[t * CORE_ROWS : (t + 1) * CORE_ROWS] for t in range(2 * TERM_DEV)], axis=1
                )
            )
        prod = jnp.dot(jnp.concatenate(halves, axis=0), rights, preferred_element_type=jnp.float32)
        return right_y, x, prod

    def store(right_y, x, prod):
        for v in range(VECS):
            for z in range(NZ):
                at = pl.multiple_of((x * VECS + v) * ROWS, ROWS)
                rows[right_y, z, pl.ds(at, ROWS)] = prod[
                    v * CORE_ROWS + z * ROWS : v * CORE_ROWS + (z + 1) * ROWS
                ]

    for side in range(2):
        load(side).wait()

        def pair(k, _):
            done = [product(side, slot_ref[side * LIST + 1 + 2 * k + n]) for n in range(2)]
            for result in done:
                store(*result)
            return 0

        lax.fori_loop(0, slot_ref[side * LIST], pair, 0)
    for y in range(NY):
        for z in range(NZ):
            out_ref[y, z] = rows[y, z].astype(jnp.bfloat16)


def part_products(slots, got, other, right):
    vmem = pl.BlockSpec(memory_space=pltpu.VMEM)
    return pl.pallas_call(
        part_kernel,
        out_shape=jax.ShapeDtypeStruct((NY, NZ, OUT_ROWS, B), jnp.bfloat16),
        in_specs=[
            pl.BlockSpec(memory_space=pltpu.SMEM),
            vmem,
            vmem,
            pl.BlockSpec(memory_space=pltpu.HBM),
        ],
        out_specs=vmem,
        scratch_shapes=[
            pltpu.VMEM((2 * NY, ENVS, B, B), jnp.bfloat16),
            pltpu.VMEM((NY, NZ, OUT_ROWS, B), jnp.float32),
            pltpu.SemaphoreType.DMA((2,)),
        ],
        compiler_params=pltpu.CompilerParams(vmem_limit_bytes=20 * 1024 * 1024),
        cost_estimate=pl.CostEstimate(
            flops=4 * NY * NX * VECS * TERM_DEV * B**3, bytes_accessed=10 * 2**20, transcendentals=0
        ),
        name="part",
    )(slots, got, other, right)


def shards(psi, left_env, right_env, left_pick, right_owner, right_pick):
    here = lax.axis_index("sec")
    rights = lax.all_gather(
        right_env.reshape(ENVS, B, B), ("sec", "term"), axis=0, tiled=False, axis_index_groups=YC_GROUPS
    )
    valid = jnp.any(right_owner.reshape(-1, PAIR_DEV) == here, axis=1)
    held = (psi, left_env.reshape(ENVS, B, B), right_owner, left_pick, right_pick)
    sent, slots = pack(*(pltpu.with_memory_space_constraint(a, pltpu.HBM) for a in held))
    got = lax.all_to_all(sent, "sec", 0, 0, tiled=True, axis_index_groups=X_GROUPS)
    other = lax.ppermute(got[:, :SWAP_ROWS], "term", CORE_SWAP)
    rights = pltpu.with_memory_space_constraint(rights, pltpu.HBM)
    both = part_products(slots, got, other, rights).reshape(NY * NZ, OUT_ROWS, B)
    both, valid = lax.optimization_barrier((both, valid))
    arrived = lax.all_to_all(both, ("sec", "term"), 0, 0, tiled=True, axis_index_groups=YZ_GROUPS)
    arrived = arrived.reshape(NY, NZ, NX, VECS, ROWS, B)
    total = jnp.sum(arrived.astype(jnp.float32), axis=1)
    total = total.transpose(2, 0, 1, 3, 4).reshape(VECS, NY * NX, ROWS, B)
    return jnp.where(valid[None, :, None, None], total, 0.0).astype(jnp.bfloat16)


def solution(mesh):
    return jax.shard_map(
        shards,
        mesh=mesh,
        in_specs=(
            P(None, "sec", None, None),
            P("term", "sec", None, None),
            P("term", "sec", None, None),
            P("sec"),
            P(),
            P(),
        ),
        out_specs=P(None, "sec", "term", None),
        check_vma=False,
    )
```

```python
import jax
import jax.numpy as jnp
from jax import lax
from jax.experimental import pallas as pl
from jax.experimental.pallas import tpu as pltpu
from jax.sharding import PartitionSpec as P

B = 128
VECS = 3
PAIR_DEV = 16
TERM_DEV = 4
NX = 4
NY = 8
NZ = 8
HALF_Y = NY // 2
ROWS = 8
CORE_ROWS = B // 2
ENVS = TERM_DEV * 2
PSI_ROWS = HALF_Y * VECS * B
ENV_ROWS = ENVS * CORE_ROWS
PICK_ROWS = 16
SWAP_ROWS = PSI_ROWS + ENV_ROWS
SENT_ROWS = SWAP_ROWS + ENV_ROWS + PICK_ROWS
OUT_ROWS = NX * VECS * ROWS
LIST = NX * HALF_Y + 2

X_GROUPS = [[y * NX + x for x in range(NX)] for y in range(NY)]
YC_GROUPS = [
    [(y * NX + x) * 2 * NZ + z * 2 + c for y in range(NY) for c in range(2)]
    for x in range(NX)
    for z in range(NZ)
]
YZ_GROUPS = [
    [(y * NX + x) * 2 * NZ + z * 2 + c for y in range(NY) for z in range(NZ)]
    for x in range(NX)
    for c in range(2)
]
CORE_SWAP = [(z * 2 + c, z * 2 + 1 - c) for z in range(NZ) for c in range(2)]


def core_rows(block, c):
    wide = block.astype(jnp.float32)
    parts = [wide[(z * 2 + c) * ROWS : (z * 2 + c + 1) * ROWS] for z in range(NZ)]
    return jnp.concatenate(parts, axis=0).astype(jnp.bfloat16)


def pack_kernel(
    psi_ref,
    left_hbm,
    owner_hbm,
    lpick_hbm,
    rpick_hbm,
    out_ref,
    slot_ref,
    left,
    owner,
    lpick,
    rpick,
    table,
    picks,
    sems,
    load_sems,
):
    here = lax.axis_index("sec")
    core = lax.axis_index("term") & 1
    loads = [
        pltpu.make_async_copy(owner_hbm, owner, load_sems.at[0]),
        pltpu.make_async_copy(left_hbm, left, load_sems.at[1]),
        pltpu.make_async_copy(lpick_hbm, lpick, load_sems.at[2]),
        pltpu.make_async_copy(rpick_hbm, rpick, load_sems.at[3]),
    ]
    for load in loads:
        load.start()
    for k in range(NX * NY):
        table[k] = 0
        picks[k] = -1
    loads[0].wait()

    def fill(j, _):
        table[owner[here * PAIR_DEV + j]] = j
        return 0

    lax.fori_loop(0, PAIR_DEV, fill, 0, unroll=True)
    copies = []
    for x in range(NX):
        for i in range(HALF_Y):
            src = table[(core * HALF_Y + i) * NX + x]
            for v in range(VECS):
                copies.append(
                    pltpu.make_async_copy(
                        psi_ref.at[v, src],
                        out_ref.at[x, pl.ds((i * VECS + v) * B, B)],
                        sems.at[len(copies)],
                    )
                )
    for copy in copies:
        copy.start()
    loads[1].wait()
    for k in range(ENVS):
        block = left[k]
        for c in range(2):
            part = core_rows(block, c)
            at = pl.multiple_of(PSI_ROWS + (1 - (core ^ c)) * ENV_ROWS + k * CORE_ROWS, CORE_ROWS)
            for x in range(NX):
                out_ref[x, pl.ds(at, CORE_ROWS)] = part
    for load in loads[2:]:
        load.wait()
    row = lax.broadcasted_iota(jnp.int32, (PICK_ROWS, B), 0)
    for x in range(NX):
        value = jnp.zeros((PICK_ROWS, B), jnp.int32)
        for y in range(NY):
            value = jnp.where(row == y, lpick[table[y * NX + x]], value)
        out_ref[x, pl.ds(SENT_ROWS - PICK_ROWS, PICK_ROWS)] = value.astype(jnp.float32).astype(jnp.bfloat16)
    my_x = here & (NX - 1)
    first = (here - my_x) * PAIR_DEV

    def slots(j, _):
        right = owner[first + j]
        slot = lax.shift_right_logical(j, 4) * NY + lax.shift_right_logical(right, 2)
        picks[jnp.where((right & (NX - 1)) == my_x, slot, NX * NY)] = rpick[first + j]
        return 0

    lax.fori_loop(0, NX * PAIR_DEV, slots, 0, unroll=8)
    for side in range(2):
        base = side * LIST

        def entry(k, count):
            y = (((core + side) & 1) * HALF_Y) + lax.shift_right_logical(k, 2)
            x = k & (NX - 1)
            pick = picks[x * NY + y]
            slot_ref[base + 1 + count] = (k * 2 + pick) & (2 * NX * HALF_Y - 1)
            return count + jnp.where(pick >= 0, 1, 0)

        count = lax.fori_loop(0, NX * HALF_Y, entry, 0, unroll=4)
        slot_ref[base] = lax.shift_right_logical(count + 1, 1)
        slot_ref[base + 1 + count] = slot_ref[base + jnp.maximum(count, 1)]
    for copy in copies:
        copy.wait()


def pack(psi, left, right_owner, left_pick, right_pick):
    hbm = pl.BlockSpec(memory_space=pltpu.HBM)
    return pl.pallas_call(
        pack_kernel,
        out_shape=(
            jax.ShapeDtypeStruct((NX, SENT_ROWS, B), jnp.bfloat16),
            jax.ShapeDtypeStruct((2 * LIST,), jnp.int32),
        ),
        in_specs=[hbm] * 5,
        out_specs=(pl.BlockSpec(memory_space=pltpu.VMEM), pl.BlockSpec(memory_space=pltpu.SMEM)),
        scratch_shapes=[
            pltpu.VMEM(left.shape, jnp.bfloat16),
            pltpu.SMEM(right_owner.shape, jnp.int32),
            pltpu.SMEM(left_pick.shape, jnp.int32),
            pltpu.SMEM(right_pick.shape, jnp.int32),
            pltpu.SMEM((NX * NY,), jnp.int32),
            pltpu.SMEM((NX * NY + 1,), jnp.int32),
            pltpu.SemaphoreType.DMA((NX * HALF_Y * VECS,)),
            pltpu.SemaphoreType.DMA((4,)),
        ],
        compiler_params=pltpu.CompilerParams(vmem_limit_bytes=16 * 1024 * 1024),
        name="pack",
    )(psi, left, right_owner, left_pick, right_pick)


def part_kernel(slot_ref, got_ref, other_ref, right_hbm, out_ref, right, rows, sems):
    core = lax.axis_index("term") & 1

    def load(side, i):
        return pltpu.make_async_copy(
            right_hbm.at[pl.ds((((core + side) & 1) * HALF_Y + i) * 2, 2)],
            right.at[pl.ds((side * HALF_Y + i) * 2, 2)],
            sems.at[side * HALF_Y + i],
        )

    for side in range(2):
        for i in range(HALF_Y):
            load(side, i).start()
    rows[...] = jnp.zeros_like(rows)
    row = lax.broadcasted_iota(jnp.int32, (PICK_ROWS, B), 0)

    def product(side, entry):
        psi_ref = (got_ref, other_ref)[side]
        pick, x, i = entry & 1, lax.shift_right_logical(entry, 1) & (NX - 1), lax.shift_right_logical(entry, 3)
        right_y = ((core + side) & 1) * HALF_Y + i
        picks = got_ref[x, pl.ds(SENT_ROWS - PICK_ROWS, PICK_ROWS), :].astype(jnp.float32)
        second = jnp.max(jnp.where(row == right_y, picks, 0.0), axis=0, keepdims=True) > 0.5
        second = jnp.broadcast_to(second, (CORE_ROWS, B))
        lefts = []
        for ref, at in ((got_ref, SWAP_ROWS), (other_ref, PSI_ROWS)):
            for t in range(TERM_DEV):
                first_env = ref[x, pl.ds(at + (t * 2) * CORE_ROWS, CORE_ROWS), :]
                second_env = ref[x, pl.ds(at + (t * 2 + 1) * CORE_ROWS, CORE_ROWS), :]
                lefts.append(jnp.where(second, second_env, first_env))
        lefts = jnp.concatenate(lefts, axis=0)
        at = (side * HALF_Y + i) * 2
        rights = jnp.concatenate(
            [right[at + c, t * 2 + pick] for c in (core, 1 - core) for t in range(TERM_DEV)], axis=0
        )
        halves = []
        for v in range(VECS):
            vec = psi_ref[x, pl.ds(pl.multiple_of((i * VECS + v) * B, B), B), :]
            half = jnp.dot(lefts, vec, preferred_element_type=jnp.float32).astype(jnp.bfloat16)
            halves.append(
                jnp.concatenate(
                    [half[t * CORE_ROWS : (t + 1) * CORE_ROWS] for t in range(2 * TERM_DEV)], axis=1
                )
            )
        prod = jnp.dot(jnp.concatenate(halves, axis=0), rights, preferred_element_type=jnp.float32)
        return right_y, x, prod

    def store(right_y, x, prod):
        for v in range(VECS):
            for z in range(NZ):
                at = pl.multiple_of((x * VECS + v) * ROWS, ROWS)
                rows[right_y, z, pl.ds(at, ROWS)] = prod[
                    v * CORE_ROWS + z * ROWS : v * CORE_ROWS + (z + 1) * ROWS
                ]

    for side in range(2):
        first = side * LIST + 1
        pairs = slot_ref[side * LIST]

        def arrive(seen, upto):
            def wait(i, _):
                load(side, i).wait()
                return 0

            lax.fori_loop(seen, upto, wait, 0)
            return jnp.maximum(seen, upto)

        def some(count, start, seen):
            entries = [slot_ref[first + start + n] for n in range(count)]
            seen = arrive(seen, lax.shift_right_logical(entries[-1], 3) + 1)
            done = [product(side, entry) for entry in entries]
            for result in done:
                store(*result)
            return seen

        fours = lax.shift_right_logical(pairs, 1)
        seen = lax.fori_loop(0, fours, lambda k, seen: some(4, 4 * k, seen), jnp.int32(0))
        seen = lax.fori_loop(0, pairs & 1, lambda k, seen: some(2, 4 * fours, seen), seen)
        arrive(seen, HALF_Y)
    for y in range(NY):
        for z in range(NZ):
            out_ref[y, z] = rows[y, z].astype(jnp.bfloat16)


def part_products(slots, got, other, right):
    vmem = pl.BlockSpec(memory_space=pltpu.VMEM)
    return pl.pallas_call(
        part_kernel,
        out_shape=jax.ShapeDtypeStruct((NY, NZ, OUT_ROWS, B), jnp.bfloat16),
        in_specs=[
            pl.BlockSpec(memory_space=pltpu.SMEM),
            vmem,
            vmem,
            pl.BlockSpec(memory_space=pltpu.HBM),
        ],
        out_specs=vmem,
        scratch_shapes=[
            pltpu.VMEM((2 * NY, ENVS, B, B), jnp.bfloat16),
            pltpu.VMEM((NY, NZ, OUT_ROWS, B), jnp.float32),
            pltpu.SemaphoreType.DMA((NY,)),
        ],
        compiler_params=pltpu.CompilerParams(vmem_limit_bytes=20 * 1024 * 1024),
        cost_estimate=pl.CostEstimate(
            flops=4 * NY * NX * VECS * TERM_DEV * B**3, bytes_accessed=10 * 2**20, transcendentals=0
        ),
        name="part",
    )(slots, got, other, right)


def shards(psi, left_env, right_env, left_pick, right_owner, right_pick):
    here = lax.axis_index("sec")
    rights = lax.all_gather(
        right_env.reshape(ENVS, B, B), ("sec", "term"), axis=0, tiled=False, axis_index_groups=YC_GROUPS
    )
    valid = jnp.any(right_owner.reshape(-1, PAIR_DEV) == here, axis=1)
    held = (psi, left_env.reshape(ENVS, B, B), right_owner, left_pick, right_pick)
    sent, slots = pack(*(pltpu.with_memory_space_constraint(a, pltpu.HBM) for a in held))
    got = lax.all_to_all(sent, "sec", 0, 0, tiled=True, axis_index_groups=X_GROUPS)
    other = lax.ppermute(got, "term", CORE_SWAP)
    rights = pltpu.with_memory_space_constraint(rights, pltpu.HBM)
    both = part_products(slots, got, other, rights).reshape(NY * NZ, OUT_ROWS, B)
    both, valid = lax.optimization_barrier((both, valid))
    arrived = lax.all_to_all(both, ("sec", "term"), 0, 0, tiled=True, axis_index_groups=YZ_GROUPS)
    arrived = arrived.reshape(NY, NZ, NX, VECS, ROWS, B)
    total = jnp.sum(arrived.astype(jnp.float32), axis=1)
    total = total.transpose(2, 0, 1, 3, 4).reshape(VECS, NY * NX, ROWS, B)
    return jnp.where(valid[None, :, None, None], total, 0.0).astype(jnp.bfloat16)


def solution(mesh):
    return jax.shard_map(
        shards,
        mesh=mesh,
        in_specs=(
            P(None, "sec", None, None),
            P("term", "sec", None, None),
            P("term", "sec", None, None),
            P("sec"),
            P(),
            P(),
        ),
        out_specs=P(None, "sec", "term", None),
        check_vma=False,
    )
```

```python
import jax
import jax.numpy as jnp
from jax import lax
from jax.experimental import pallas as pl
from jax.experimental.pallas import tpu as pltpu
from jax.sharding import PartitionSpec as P

B = 128
VECS = 3
PAIR_DEV = 16
TERM_DEV = 4
NX = 4
NY = 8
NZ = 8
HALF_Y = NY // 2
ROWS = 8
CORE_ROWS = B // 2
ENVS = TERM_DEV * 2
PSI_ROWS = HALF_Y * VECS * B
ENV_ROWS = ENVS * CORE_ROWS
PICK_ROWS = 16
SWAP_ROWS = PSI_ROWS + ENV_ROWS
SENT_ROWS = SWAP_ROWS + ENV_ROWS + PICK_ROWS
OUT_ROWS = NX * VECS * ROWS
LIST = NX * HALF_Y + 2

X_GROUPS = [[y * NX + x for x in range(NX)] for y in range(NY)]
YC_GROUPS = [
    [(y * NX + x) * 2 * NZ + z * 2 + c for y in range(NY) for c in range(2)]
    for x in range(NX)
    for z in range(NZ)
]
YZ_GROUPS = [
    [(y * NX + x) * 2 * NZ + z * 2 + c for y in range(NY) for z in range(NZ)]
    for x in range(NX)
    for c in range(2)
]
CORE_SWAP = [(z * 2 + c, z * 2 + 1 - c) for z in range(NZ) for c in range(2)]


def core_rows(block, c):
    wide = block.astype(jnp.float32)
    parts = [wide[(z * 2 + c) * ROWS : (z * 2 + c + 1) * ROWS] for z in range(NZ)]
    return jnp.concatenate(parts, axis=0).astype(jnp.bfloat16)


def pack_kernel(
    psi_ref,
    left_hbm,
    owner_hbm,
    lpick_hbm,
    rpick_hbm,
    out_ref,
    slot_ref,
    left,
    owner,
    lpick,
    rpick,
    table,
    picks,
    sems,
    load_sems,
):
    here = lax.axis_index("sec")
    core = lax.axis_index("term") & 1
    loads = [
        pltpu.make_async_copy(owner_hbm, owner, load_sems.at[0]),
        pltpu.make_async_copy(left_hbm, left, load_sems.at[1]),
        pltpu.make_async_copy(lpick_hbm, lpick, load_sems.at[2]),
        pltpu.make_async_copy(rpick_hbm, rpick, load_sems.at[3]),
    ]
    for load in loads:
        load.start()
    for k in range(NX * NY):
        table[k] = 0
        picks[k] = -1
    loads[0].wait()

    def fill(j, _):
        table[owner[here * PAIR_DEV + j]] = j
        return 0

    lax.fori_loop(0, PAIR_DEV, fill, 0, unroll=True)
    copies = []
    for x in range(NX):
        for i in range(HALF_Y):
            src = table[(core * HALF_Y + i) * NX + x]
            for v in range(VECS):
                copies.append(
                    pltpu.make_async_copy(
                        psi_ref.at[v, src],
                        out_ref.at[x, pl.ds((i * VECS + v) * B, B)],
                        sems.at[len(copies)],
                    )
                )
    for copy in copies:
        copy.start()
    loads[1].wait()
    for k in range(ENVS):
        block = left[k]
        for c in range(2):
            part = core_rows(block, c)
            at = pl.multiple_of(PSI_ROWS + (1 - (core ^ c)) * ENV_ROWS + k * CORE_ROWS, CORE_ROWS)
            for x in range(NX):
                out_ref[x, pl.ds(at, CORE_ROWS)] = part
    for load in loads[2:]:
        load.wait()
    row = lax.broadcasted_iota(jnp.int32, (PICK_ROWS, B), 0)
    for x in range(NX):
        value = jnp.zeros((PICK_ROWS, B), jnp.int32)
        for y in range(NY):
            value = jnp.where(row == y, lpick[table[y * NX + x]], value)
        out_ref[x, pl.ds(SENT_ROWS - PICK_ROWS, PICK_ROWS)] = value.astype(jnp.float32).astype(jnp.bfloat16)
    my_x = here & (NX - 1)
    first = (here - my_x) * PAIR_DEV

    def slots(j, _):
        right = owner[first + j]
        slot = lax.shift_right_logical(j, 4) * NY + lax.shift_right_logical(right, 2)
        picks[jnp.where((right & (NX - 1)) == my_x, slot, NX * NY)] = rpick[first + j]
        return 0

    lax.fori_loop(0, NX * PAIR_DEV, slots, 0, unroll=True)
    for side in range(2):
        base = side * LIST

        def entry(k, count):
            y = (((core + side) & 1) * HALF_Y) + lax.shift_right_logical(k, 2)
            x = k & (NX - 1)
            pick = picks[x * NY + y]
            slot_ref[base + 1 + count] = (k * 2 + pick) & (2 * NX * HALF_Y - 1)
            return count + jnp.where(pick >= 0, 1, 0)

        count = lax.fori_loop(0, NX * HALF_Y, entry, 0, unroll=True)
        slot_ref[base] = lax.shift_right_logical(count + 1, 1)
        slot_ref[base + 1 + count] = slot_ref[base + jnp.maximum(count, 1)]
    for copy in copies:
        copy.wait()


def pack(psi, left, right_owner, left_pick, right_pick):
    hbm = pl.BlockSpec(memory_space=pltpu.HBM)
    return pl.pallas_call(
        pack_kernel,
        out_shape=(
            jax.ShapeDtypeStruct((NX, SENT_ROWS, B), jnp.bfloat16),
            jax.ShapeDtypeStruct((2 * LIST,), jnp.int32),
        ),
        in_specs=[hbm] * 5,
        out_specs=(pl.BlockSpec(memory_space=pltpu.VMEM), pl.BlockSpec(memory_space=pltpu.SMEM)),
        scratch_shapes=[
            pltpu.VMEM(left.shape, jnp.bfloat16),
            pltpu.SMEM(right_owner.shape, jnp.int32),
            pltpu.SMEM(left_pick.shape, jnp.int32),
            pltpu.SMEM(right_pick.shape, jnp.int32),
            pltpu.SMEM((NX * NY,), jnp.int32),
            pltpu.SMEM((NX * NY + 1,), jnp.int32),
            pltpu.SemaphoreType.DMA((NX * HALF_Y * VECS,)),
            pltpu.SemaphoreType.DMA((4,)),
        ],
        compiler_params=pltpu.CompilerParams(vmem_limit_bytes=16 * 1024 * 1024),
        name="pack",
    )(psi, left, right_owner, left_pick, right_pick)


def part_kernel(slot_ref, got_ref, other_ref, right_hbm, out_ref, right, rows, sems):
    core = lax.axis_index("term") & 1

    def load(side, i):
        return pltpu.make_async_copy(
            right_hbm.at[pl.ds((((core + side) & 1) * HALF_Y + i) * 2, 2)],
            right.at[pl.ds((side * HALF_Y + i) * 2, 2)],
            sems.at[side * HALF_Y + i],
        )

    for side in range(2):
        for i in range(HALF_Y):
            load(side, i).start()
    rows[...] = jnp.zeros_like(rows)
    row = lax.broadcasted_iota(jnp.int32, (PICK_ROWS, B), 0)

    def product(side, entry):
        psi_ref = (got_ref, other_ref)[side]
        pick, x, i = entry & 1, lax.shift_right_logical(entry, 1) & (NX - 1), lax.shift_right_logical(entry, 3)
        right_y = ((core + side) & 1) * HALF_Y + i
        picks = got_ref[x, pl.ds(SENT_ROWS - PICK_ROWS, PICK_ROWS), :].astype(jnp.float32)
        second = jnp.max(jnp.where(row == right_y, picks, 0.0), axis=0, keepdims=True) > 0.5
        second = jnp.broadcast_to(second, (CORE_ROWS, B))
        lefts = []
        for ref, at in ((got_ref, SWAP_ROWS), (other_ref, PSI_ROWS)):
            for t in range(TERM_DEV):
                first_env = ref[x, pl.ds(at + (t * 2) * CORE_ROWS, CORE_ROWS), :]
                second_env = ref[x, pl.ds(at + (t * 2 + 1) * CORE_ROWS, CORE_ROWS), :]
                lefts.append(jnp.where(second, second_env, first_env))
        lefts = jnp.concatenate(lefts, axis=0)
        at = (side * HALF_Y + i) * 2
        rights = jnp.concatenate(
            [right[at + c, t * 2 + pick] for c in (core, 1 - core) for t in range(TERM_DEV)], axis=0
        )
        halves = []
        for v in range(VECS):
            vec = psi_ref[x, pl.ds(pl.multiple_of((i * VECS + v) * B, B), B), :]
            half = jnp.dot(lefts, vec, preferred_element_type=jnp.float32).astype(jnp.bfloat16)
            halves.append(
                jnp.concatenate(
                    [half[t * CORE_ROWS : (t + 1) * CORE_ROWS] for t in range(2 * TERM_DEV)], axis=1
                )
            )
        prod = jnp.dot(jnp.concatenate(halves, axis=0), rights, preferred_element_type=jnp.float32)
        return right_y, x, prod

    def store(right_y, x, prod):
        for v in range(VECS):
            for z in range(NZ):
                at = pl.multiple_of((x * VECS + v) * ROWS, ROWS)
                rows[right_y, z, pl.ds(at, ROWS)] = prod[
                    v * CORE_ROWS + z * ROWS : v * CORE_ROWS + (z + 1) * ROWS
                ]

    for side in range(2):
        first = side * LIST + 1
        pairs = slot_ref[side * LIST]

        def arrive(seen, upto):
            def wait(i, _):
                load(side, i).wait()
                return 0

            lax.fori_loop(seen, upto, wait, 0)
            return jnp.maximum(seen, upto)

        def some(count, start, seen):
            entries = [slot_ref[first + start + n] for n in range(count)]
            seen = arrive(seen, lax.shift_right_logical(entries[-1], 3) + 1)
            done = [product(side, entry) for entry in entries]
            for result in done:
                store(*result)
            return seen

        fours = lax.shift_right_logical(pairs, 1)
        seen = lax.fori_loop(0, fours, lambda k, seen: some(4, 4 * k, seen), jnp.int32(0))
        seen = lax.fori_loop(0, pairs & 1, lambda k, seen: some(2, 4 * fours, seen), seen)
        arrive(seen, HALF_Y)
    for y in range(NY):
        for z in range(NZ):
            out_ref[y, z] = rows[y, z].astype(jnp.bfloat16)


def part_products(slots, got, other, right):
    vmem = pl.BlockSpec(memory_space=pltpu.VMEM)
    return pl.pallas_call(
        part_kernel,
        out_shape=jax.ShapeDtypeStruct((NY, NZ, OUT_ROWS, B), jnp.bfloat16),
        in_specs=[
            pl.BlockSpec(memory_space=pltpu.SMEM),
            vmem,
            vmem,
            pl.BlockSpec(memory_space=pltpu.HBM),
        ],
        out_specs=vmem,
        scratch_shapes=[
            pltpu.VMEM((2 * NY, ENVS, B, B), jnp.bfloat16),
            pltpu.VMEM((NY, NZ, OUT_ROWS, B), jnp.float32),
            pltpu.SemaphoreType.DMA((NY,)),
        ],
        compiler_params=pltpu.CompilerParams(vmem_limit_bytes=20 * 1024 * 1024),
        cost_estimate=pl.CostEstimate(
            flops=4 * NY * NX * VECS * TERM_DEV * B**3, bytes_accessed=10 * 2**20, transcendentals=0
        ),
        name="part",
    )(slots, got, other, right)


def shards(psi, left_env, right_env, left_pick, right_owner, right_pick):
    here = lax.axis_index("sec")
    rights = lax.all_gather(
        right_env.reshape(ENVS, B, B), ("sec", "term"), axis=0, tiled=False, axis_index_groups=YC_GROUPS
    )
    valid = jnp.any(right_owner.reshape(-1, PAIR_DEV) == here, axis=1)
    held = (psi, left_env.reshape(ENVS, B, B), right_owner, left_pick, right_pick)
    sent, slots = pack(*(pltpu.with_memory_space_constraint(a, pltpu.HBM) for a in held))
    got = lax.all_to_all(sent, "sec", 0, 0, tiled=True, axis_index_groups=X_GROUPS)
    other = lax.ppermute(got, "term", CORE_SWAP)
    rights = pltpu.with_memory_space_constraint(rights, pltpu.HBM)
    both = part_products(slots, got, other, rights).reshape(NY * NZ, OUT_ROWS, B)
    both, valid = lax.optimization_barrier((both, valid))
    arrived = lax.all_to_all(both, ("sec", "term"), 0, 0, tiled=True, axis_index_groups=YZ_GROUPS)
    arrived = arrived.reshape(NY, NZ, NX, VECS, ROWS, B)
    total = jnp.sum(arrived.astype(jnp.float32), axis=1)
    total = total.transpose(2, 0, 1, 3, 4).reshape(VECS, NY * NX, ROWS, B)
    return jnp.where(valid[None, :, None, None], total, 0.0).astype(jnp.bfloat16)


def solution(mesh):
    return jax.shard_map(
        shards,
        mesh=mesh,
        in_specs=(
            P(None, "sec", None, None),
            P("term", "sec", None, None),
            P("term", "sec", None, None),
            P("sec"),
            P(),
            P(),
        ),
        out_specs=P(None, "sec", "term", None),
        check_vma=False,
    )
```
